32 devices in a mesh: chan: 8 (over z, y), vox: 4 (over x, core).
Axes of the slice: x: 2, y: 2, z: 4, core: 2. Of those that a mesh axis runs over, the one named last changes fastest.
Arguments:
- spectra: bfloat16 [2, 512, 2048], P(None, ('chan', 'vox')), may hold values from -6 to 6
- pair_mask: int32 [8, 2], P('chan'), may hold values 0 or 1
- send_rows: int32 [32, 2, 32, 32], P(('chan', 'vox')), may hold values from 0 to 1023
- footprint: int32 [8192, 4, 8], P(('chan', 'vox')), may hold values from 0 to 2047
- kernels: bfloat16 [4, 512, 256], replicated, may hold values from -0.125 to 0.125
Outputs:
- power_map: float32 [8192, 256], P(('chan', 'vox'))
The draws below stay inside these ranges and needn't reach their ends.
Inputs may be any that keep to these rules, and one draw needn't show every extreme that they name: `send_rows`: local lag-row indices of one offset on the sending device. `footprint`: slots of the receiving device, numbered (offset 32 + sender) * 32 + slot.
All inputs are finite; a program needn't handle non-finite values. No bound on the sum of `pair_mask` on one device may be relied on, other than what follows from the above.
Results may differ from the reference program's by a relative error of at most 0.015.
Values may be sent and summed in bfloat16 or wider, within the bound.
A program may use at most 64 MiB of HBM per device.

```python
import math
import jax
import jax.numpy as jnp
from jax import lax

F = 2048
LAG = 512
TILE = 256
KINDS = 4
SLOTS = 8
BAND = 2
CH_DEV = 16
TILES_DEV = 256
CHANNELS = 512
BLOCK = 64
BLOCKS = 8
PAIR_ROWS = 1024
CAP = 32
RECEIVED = 2048
TILES = 8192
N_CHAN = 8
N_VOX = 4
DEVICES = 32


def touch_ends(array, rng, smallest, largest):
    shape = array.shape
    index_at = [jax.random.randint(jax.random.fold_in(rng, axis), (), 0, shape[axis]) for axis in range(len(shape))]
    array = array.at[tuple(index_at)].set(smallest)
    longest = shape.index(max(shape))
    index_at[longest] = (index_at[longest] + 1) % shape[longest]
    return array.at[tuple(index_at)].set(largest)


def block_scale(stream_key, shape, pieces, least, top_value):
    gain, own = 1.0, jax.random.fold_in(stream_key, 6)
    for position, blocks in pieces:
        draws = jnp.exp(jax.random.uniform(jax.random.fold_in(own, position), (blocks,), jnp.float32, least / len(pieces), top_value / len(pieces)))
        gain = gain * jnp.repeat(draws, shape[position] // blocks).reshape([-1 if axis == position else 1 for axis in range(len(shape))])
    return gain


def centred(rng, shape, deviation, most, cuts=(), kind=jnp.bfloat16):
    loudness = block_scale(rng, shape, cuts, -0.22, 0.18) if cuts else 1.0
    entries = jax.random.normal(rng, shape, jnp.float32) * deviation * loudness
    return jnp.minimum(jnp.maximum(entries, -most), most).astype(kind)


def setup_inputs(seed: int = 0) -> dict:
    key_of = jax.random.split(jax.random.key(seed), 6)
    spectra = centred(key_of[0], (2, CHANNELS, F), 1.0, 6.0, ((1, 32),))
    pair_mask = touch_ends((jax.random.randint(key_of[1], (BLOCKS, BAND), 0, 4) < 3).astype(jnp.int32), jax.random.fold_in(key_of[1], 1), 0, 1)
    send_rows = touch_ends(jax.random.randint(key_of[2], (DEVICES, BAND, DEVICES, CAP), 0, PAIR_ROWS), jax.random.fold_in(key_of[2], 1), 0, PAIR_ROWS - 1).astype(jnp.int32)
    footprint = touch_ends(jax.random.randint(key_of[3], (TILES, KINDS, SLOTS), 0, RECEIVED), jax.random.fold_in(key_of[3], 1), 0, RECEIVED - 1).astype(jnp.int32)
    kernels = centred(key_of[4], (KINDS, LAG, TILE), (KINDS * LAG) ** -0.5, 0.125)
    return dict(spectra=spectra, pair_mask=pair_mask, send_rows=send_rows, footprint=footprint, kernels=kernels)


def whiten(spectra):
    real_part = spectra[0].astype(jnp.float32)
    imag_part = spectra[1].astype(jnp.float32)
    inverse_mag = 1.0 / jnp.sqrt(real_part * real_part + imag_part * imag_part + 0.25)
    return jnp.stack([real_part * inverse_mag, imag_part * inverse_mag]).astype(jnp.bfloat16)

def phase_table(bins, lags):
    bin_index = jnp.arange(bins, dtype=jnp.int32)[:, None]
    lag_index = jnp.arange(lags, dtype=jnp.int32)[None, :] - lags // 2
    phase_index = bin_index * lag_index % bins
    angles = phase_index.astype(jnp.float32) * (2.0 * math.pi / bins)
    norm_factor = 1.0 / math.sqrt(bins)
    return jnp.concatenate([jnp.cos(angles) * norm_factor, -jnp.sin(angles) * norm_factor], 0).astype(jnp.bfloat16)

def form_lags(first_set, second_set, lag_table):
    first_real = first_set[0].astype(jnp.float32)[:, None, :]
    first_imag = first_set[1].astype(jnp.float32)[:, None, :]
    second_real = second_set[0].astype(jnp.float32)[None, :, :]
    second_imag = second_set[1].astype(jnp.float32)[None, :, :]
    cross_real = first_real * second_real + first_imag * second_imag
    cross_imag = first_imag * second_real - first_real * second_imag
    stacked = jnp.concatenate([cross_real, cross_imag], -1).astype(jnp.bfloat16)
    stacked = stacked.reshape(-1, stacked.shape[-1])
    return jnp.dot(stacked.astype(jnp.float32), lag_table.astype(jnp.float32), preferred_element_type=jnp.float32)

def reference(spectra, pair_mask, send_rows, footprint, kernels):
    whitened = whiten(spectra)
    lag_table = phase_table(F, LAG)
    devices_all = N_CHAN * N_VOX

    def device_lags(source):
        owner = source // N_VOX
        first_set = lax.dynamic_slice_in_dim(whitened, source * CH_DEV, CH_DEV, 1)
        produced = []
        for offset in range(BAND):
            partner = (owner + offset + 1) % N_CHAN
            second_set = lax.dynamic_slice_in_dim(whitened, partner * BLOCK, BLOCK, 1)
            weight = pair_mask[owner, offset].astype(jnp.float32)
            produced.append((form_lags(first_set, second_set, lag_table) * weight).astype(jnp.bfloat16))
        return jnp.stack(produced)
    all_lags = lax.map(device_lags, jnp.arange(devices_all, dtype=jnp.int32))
    source_ids = jnp.arange(devices_all, dtype=jnp.int32)[:, None, None]
    offset_ids = jnp.arange(BAND, dtype=jnp.int32)[None, :, None]

    def tile_power(target):
        chosen = lax.dynamic_index_in_dim(send_rows, target, 2, keepdims=False)
        arrived = all_lags[source_ids, offset_ids, chosen]
        flattened = jnp.transpose(arrived, (1, 0, 2, 3)).reshape(-1, LAG)
        tile_feet = lax.dynamic_slice_in_dim(footprint, target * TILES_DEV, TILES_DEV, 0)
        picked = flattened[tile_feet]
        summed = lax.optimization_barrier(jnp.sum(picked.astype(jnp.float32), axis=2)).astype(jnp.bfloat16)
        return jnp.einsum('tmk,mkv->tv', summed.astype(jnp.float32), kernels.astype(jnp.float32))
    powers = lax.map(tile_power, jnp.arange(devices_all, dtype=jnp.int32))
    return powers.reshape(TILES, TILE)
```

```python
import functools
import math

import jax
import jax.numpy as jnp
import numpy as np
from jax import lax
from jax.experimental import pallas as pl
from jax.experimental.pallas import tpu as pltpu
from jax.sharding import PartitionSpec as P

MESH = pl.DeviceIdType.MESH
LANES = 128


def whiten(spectra):
    real_part = spectra[0].astype(jnp.float32)
    imag_part = spectra[1].astype(jnp.float32)
    inverse_mag = 1.0 / jnp.sqrt(real_part * real_part + imag_part * imag_part + 0.25)
    return jnp.stack([real_part * inverse_mag, imag_part * inverse_mag]).astype(jnp.bfloat16)


def phase_table(bins, lags):
    bin_index = np.arange(bins, dtype=np.int64)[:, None]
    lag_index = np.arange(lags, dtype=np.int64)[None, :] - lags // 2
    phase_index = bin_index * lag_index % bins
    angles = phase_index.astype(np.float32) * np.float32(2.0 * math.pi / bins)
    norm_factor = np.float32(1.0 / math.sqrt(bins))
    table = np.concatenate([np.cos(angles) * norm_factor, -np.sin(angles) * norm_factor], 0)
    return jnp.asarray(table.astype(jnp.bfloat16))


def kernel(dims, own, feet, table_hbm, kern, out, held, table, counts, lags, send_sem, recv_sem, load_sem):
    n_chan, n_vox, per_dev, bins, offsets, cap = dims
    n_dev = n_chan * n_vox
    depth = n_chan // 2
    chan, vox = lax.axis_index("chan"), lax.axis_index("vox")
    hi, lo = chan // 2, chan % 2
    far, core = vox // 2, vox % 2
    me = chan * n_vox + vox

    def chan_at(d, flip):
        l = 1 - lo if flip else lo
        return lax.rem(hi + depth - d, depth) * 2 + l

    def vox_at(flip_x, flip_core):
        f = 1 - far if flip_x else far
        c = 1 - core if flip_core else core
        return f * 2 + c

    def source(d, flip_y, flip_x, flip_core):
        return chan_at(d, flip_y) * n_vox + vox_at(flip_x, flip_core)

    load = pltpu.make_async_copy(table_hbm, table, load_sem)
    load.start()

    barrier = pltpu.get_barrier_semaphore()
    near_y = (chan_at(0, True), vox)
    near_x = (chan, vox_at(True, False))
    near_core = (chan, vox_at(False, True))
    column = [(chan_at(depth - d, False), vox) for d in range(1, depth)]
    partners = column + [near_y, near_x, near_core]
    for device in partners:
        pl.semaphore_signal(barrier, inc=1, device_id=device, device_id_type=MESH)
    held[0, me] = own[0]
    held[1, me] = own[1]
    pl.semaphore_wait(barrier, len(partners))

    started = []

    def send(part, shard, device):
        slot = sum(1 for p, _ in started if p == part)
        copy = pltpu.make_async_remote_copy(
            src_ref=held.at[part, shard],
            dst_ref=held.at[part, shard],
            send_sem=send_sem.at[part, slot],
            recv_sem=recv_sem.at[part, shard],
            device_id=device,
            device_id_type=MESH,
        )
        copy.start()
        started.append((part, copy))

    def arrive(part, shard):
        pltpu.make_async_remote_copy(
            src_ref=held.at[part, shard],
            dst_ref=held.at[part, shard],
            send_sem=send_sem.at[part, 0],
            recv_sem=recv_sem.at[part, shard],
            device_id=near_core,
            device_id_type=MESH,
        ).wait_recv()

    rows_out, slots = feet.shape
    received = counts.shape[1]
    pieces = 4 * depth
    piece_rows = rows_out // pieces

    def count_piece(step):
        start = step * piece_rows
        slot_id = lax.broadcasted_iota(jnp.int32, (piece_rows, received), 1)
        total = jnp.zeros((piece_rows, received), jnp.float32)
        for slot in range(slots):
            total += jnp.where(slot_id == feet[pl.ds(start, piece_rows), slot : slot + 1], 1.0, 0.0)
        counts[pl.ds(start, piece_rows), :] = total.astype(jnp.bfloat16)

    first = (near_y, near_x)
    second = (near_x, near_y)
    for d in range(depth):
        for part in range(2):
            shard = source(d, False, False, False)
            if d > 0:
                arrive(part, shard)
            else:
                for device in column:
                    send(part, shard, device)
            send(part, shard, first[part])
            send(part, shard, second[part])
            send(part, shard, near_core)
        count_piece(d)
    for d in range(depth):
        for part in range(2):
            shard = source(d, part == 0, part == 1, False)
            arrive(part, shard)
            send(part, shard, second[part])
            send(part, shard, near_core)
        count_piece(depth + d)
    for d in range(depth):
        for part in range(2):
            shard = source(d, part == 1, part == 0, False)
            arrive(part, shard)
            send(part, shard, near_core)
        count_piece(2 * depth + d)
    for d in range(depth):
        for part in range(2):
            shard = source(d, True, True, False)
            arrive(part, shard)
            send(part, shard, near_core)
        count_piece(3 * depth + d)
    load.wait()
    for flip_y, flip_x in ((False, False), (True, False), (False, True), (True, True)):
        for d in range(depth):
            for part in range(2):
                arrive(part, source(d, flip_y, flip_x, True))
    for _, copy in started:
        copy.wait_send()

    per_receiver = offsets * cap
    in_row = LANES // per_receiver
    my_row, my_lane = me // in_row, lax.rem(me, in_row) * per_receiver
    block = n_vox * per_dev
    rows = n_vox * cap
    chunk = 512

    def numbers(part, b, k):
        tiles = held[part, pl.ds(b * n_vox, n_vox), :, bins:].astype(jnp.float32)
        row_id = lax.broadcasted_iota(jnp.int32, tiles.shape, 1)
        line = jnp.sum(jnp.where(row_id == my_row, tiles, 0.0), axis=1, keepdims=True)
        shape = (n_vox, cap, LANES)
        lane = lax.broadcasted_iota(jnp.int32, shape, 2)
        wanted = lax.broadcasted_iota(jnp.int32, shape, 1) + (my_lane + k * cap)
        picked = jnp.where(lane == wanted, jnp.broadcast_to(line, shape), 0.0)
        return jnp.sum(picked, axis=2, keepdims=True)

    def one_hot(values):
        chosen = lax.broadcasted_iota(jnp.int32, (n_vox, cap, block), 2).astype(jnp.float32)
        hot = jnp.where(chosen == values, 1.0, 0.0)
        return hot.reshape(rows, block).astype(jnp.bfloat16)

    def select(hot, part, b, at):
        channels = held[part, pl.ds(b * n_vox, n_vox), :, at : at + chunk].reshape(block, chunk)
        return jnp.dot(hot, channels, preferred_element_type=jnp.float32)

    def one_block(b, carry):
        owner = lax.broadcasted_iota(jnp.int32, (n_vox, cap, 1), 0).astype(jnp.float32) * per_dev
        mine, theirs, partner = [], [], []
        for k in range(offsets):
            mine.append(one_hot(numbers(0, b, k) + owner))
            theirs.append(one_hot(numbers(1, b, k)))
            partner.append(lax.rem(b + k + 1, n_chan))
        both = jnp.concatenate(mine, 0)
        total = jnp.zeros((offsets * rows, table.shape[1]), jnp.float32)
        for at in range(0, bins, chunk):
            re_i, im_i = select(both, 0, b, at), select(both, 1, b, at)
            re_j = jnp.concatenate([select(theirs[k], 0, partner[k], at) for k in range(offsets)], 0)
            im_j = jnp.concatenate([select(theirs[k], 1, partner[k], at) for k in range(offsets)], 0)
            cross_re = (re_i * re_j + im_i * im_j).astype(jnp.bfloat16)
            cross_im = (im_i * re_j - re_i * im_j).astype(jnp.bfloat16)
            total += jnp.dot(cross_re, table[at : at + chunk], preferred_element_type=jnp.float32)
            total += jnp.dot(
                cross_im, table[bins + at : bins + at + chunk], preferred_element_type=jnp.float32
            )
        for k in range(offsets):
            place = pl.multiple_of(k * n_dev * cap + b * rows, rows)
            lags[pl.ds(place, rows), :] = total[k * rows : (k + 1) * rows].astype(jnp.bfloat16)
        return carry

    lax.fori_loop(0, n_chan, one_block, 0)

    tiles = out.shape[0]
    power = jnp.zeros(out.shape, jnp.float32)
    for kind in range(kern.shape[0]):
        summed = jnp.dot(
            counts[kind * tiles : (kind + 1) * tiles], lags[...], preferred_element_type=jnp.float32
        ).astype(jnp.bfloat16)
        power += jnp.dot(summed, kern[kind], preferred_element_type=jnp.float32)
    out[...] = power


def local(spectra, pair_mask, send_rows, footprint, kernels):
    n_chan, n_vox = lax.axis_size("chan"), lax.axis_size("vox")
    n_dev = n_chan * n_vox
    _, per_dev, bins = spectra.shape
    kinds, lag_count, voxels = kernels.shape
    _, offsets, _, cap = send_rows.shape
    tiles, _, slots = footprint.shape
    block = n_vox * per_dev
    table = phase_table(bins, lag_count)
    order = jnp.transpose(send_rows[0], (1, 0, 2))
    own_channel = jnp.where(pair_mask[0][None, :, None] > 0, order // block, -128)
    numbers = jnp.stack([own_channel, order % block]).reshape(2, per_dev, -1)
    shard = jnp.concatenate([whiten(spectra), numbers.astype(jnp.bfloat16)], -1)
    width = shard.shape[-1]
    feet = jnp.transpose(footprint, (1, 0, 2)).reshape(kinds * tiles, slots)
    received = offsets * n_dev * cap
    sends = 4 * n_chan // 2 * 2 + n_chan * 2
    vmem = pl.BlockSpec(memory_space=pltpu.VMEM)
    return pl.pallas_call(
        functools.partial(kernel, (n_chan, n_vox, per_dev, bins, offsets, cap)),
        out_shape=jax.ShapeDtypeStruct((tiles, voxels), jnp.float32),
        in_specs=[vmem, vmem, pl.BlockSpec(memory_space=pl.ANY), vmem],
        out_specs=vmem,
        scratch_shapes=[
            pltpu.VMEM((2, n_dev, per_dev, width), jnp.bfloat16),
            pltpu.VMEM(table.shape, jnp.bfloat16),
            pltpu.VMEM((kinds * tiles, received), jnp.bfloat16),
            pltpu.VMEM((received, lag_count), jnp.bfloat16),
            pltpu.SemaphoreType.DMA((2, sends)),
            pltpu.SemaphoreType.DMA((2, n_dev)),
            pltpu.SemaphoreType.DMA,
        ],
        compiler_params=pltpu.CompilerParams(
            collective_id=0, has_side_effects=True, vmem_limit_bytes=56 * 1024 * 1024
        ),
    )(shard, feet, table, kernels)


def solution(mesh):
    return jax.shard_map(
        local,
        mesh=mesh,
        in_specs=(
            P(None, ("chan", "vox"), None),
            P("chan", None),
            P(("chan", "vox"), None, None, None),
            P(("chan", "vox"), None, None),
            P(),
        ),
        out_specs=P(("chan", "vox"), None),
        check_vma=False,
    )
```

```python
import functools
import math

import jax
import jax.numpy as jnp
import numpy as np
from jax import lax
from jax.experimental import pallas as pl
from jax.experimental.pallas import tpu as pltpu
from jax.sharding import PartitionSpec as P

MESH = pl.DeviceIdType.MESH
LANES = 128


def whiten(spectra):
    real_part = spectra[0].astype(jnp.float32)
    imag_part = spectra[1].astype(jnp.float32)
    inverse_mag = 1.0 / jnp.sqrt(real_part * real_part + imag_part * imag_part + 0.25)
    return jnp.stack([real_part * inverse_mag, imag_part * inverse_mag]).astype(jnp.bfloat16)


def phase_table(bins, lags):
    bin_index = np.arange(bins, dtype=np.int64)[:, None]
    lag_index = np.arange(lags, dtype=np.int64)[None, :] - lags // 2
    phase_index = bin_index * lag_index % bins
    angles = phase_index.astype(np.float32) * np.float32(2.0 * math.pi / bins)
    norm_factor = np.float32(1.0 / math.sqrt(bins))
    table = np.concatenate([np.cos(angles) * norm_factor, -np.sin(angles) * norm_factor], 0)
    return jnp.asarray(table.astype(jnp.bfloat16))


def kernel(dims, *refs):
    n_chan, n_vox, per_dev, bins, offsets, cap, stages = dims
    own, refs = refs[:stages], refs[stages:]
    feet, table_hbm, out = refs[:3]
    held, refs = refs[3 : 3 + stages], refs[3 + stages :]
    table, counts, lags, partial, feet_rows, hot_i, hot_j, send_sem, recv_sem, load_sem = refs
    n_dev = n_chan * n_vox
    depth = n_chan // 2
    width = bins // stages
    chan, vox = lax.axis_index("chan"), lax.axis_index("vox")
    hi, lo = chan // 2, chan % 2
    far, core = vox // 2, vox % 2
    me = chan * n_vox + vox

    def chan_at(d, flip):
        l = 1 - lo if flip else lo
        return lax.rem(hi + depth - d, depth) * 2 + l

    def vox_at(flip_x, flip_core):
        f = 1 - far if flip_x else far
        c = 1 - core if flip_core else core
        return f * 2 + c

    def source(d, flip_y, flip_x, flip_core):
        return chan_at(d, flip_y) * n_vox + vox_at(flip_x, flip_core)

    barrier = pltpu.get_barrier_semaphore()
    near_y = (chan_at(0, True), vox)
    near_x = (chan, vox_at(True, False))
    near_core = (chan, vox_at(False, True))
    column = [(chan_at(depth - d, False), vox) for d in range(1, depth)]
    partners = column + [near_y, near_x, near_core]
    for device in partners:
        pl.semaphore_signal(barrier, inc=1, device_id=device, device_id_type=MESH)
    for stage in range(stages):
        for part in range(2):
            held[stage][part, me] = own[stage][part]
    load = pltpu.make_async_copy(table_hbm, table, load_sem)
    load.start()
    pl.semaphore_wait(barrier, len(partners))

    first = (near_y, near_x)
    second = (near_x, near_y)

    def copy(stage, part, shard, device, slot):
        return pltpu.make_async_remote_copy(
            src_ref=held[stage].at[part, shard],
            dst_ref=held[stage].at[part, shard],
            send_sem=send_sem.at[stage * 2 + part, slot],
            recv_sem=recv_sem.at[stage * 2 + part, shard],
            device_id=device,
            device_id_type=MESH,
        )

    def spread(stage, part, phase, d, shard):
        if phase == 0:
            copy(stage, part, shard, first[part], d).start()
            copy(stage, part, shard, second[part], depth + d).start()
        if phase == 1:
            copy(stage, part, shard, second[part], 2 * depth + d).start()
        copy(stage, part, shard, near_core, (3 + phase) * depth + d).start()

    def send_own(stage):
        for part in range(2):
            for d, device in enumerate(column):
                copy(stage, part, me, device, 7 * depth + d).start()
        for part in range(2):
            spread(stage, part, 0, 0, me)

    def pass_on(stage, phase, d):
        for part in range(2):
            flip_y = phase == 3 or phase == 1 + part
            flip_x = phase == 3 or phase == 2 - part
            shard = source(d, flip_y, flip_x, False)
            copy(stage, part, shard, near_core, 0).wait_recv()
            spread(stage, part, phase, d, shard)

    def finish_arrivals(stage):
        for flip_y, flip_x in ((False, False), (True, False), (False, True), (True, True)):
            def one(d, carry):
                for part in range(2):
                    shard = source(d, flip_y, flip_x, True)
                    copy(stage, part, shard, near_core, 0).wait_recv()
                return carry
            lax.fori_loop(0, depth, one, 0)

    rows_out, slots = feet_rows.shape
    kinds, tiles = feet.shape[0], feet.shape[2]
    received = counts.shape[1]
    pieces = 4 * depth
    piece_rows = rows_out // pieces

    def count_piece(step):
        start = pl.multiple_of(step * piece_rows, piece_rows)
        slot_id = lax.broadcasted_iota(jnp.int32, (piece_rows, received), 1)
        total = jnp.zeros((piece_rows, received), jnp.float32)
        for slot in range(slots):
            total += jnp.where(slot_id == feet_rows[pl.ds(start, piece_rows), slot : slot + 1], 1.0, 0.0)
        counts[pl.ds(start, piece_rows), :] = total.astype(jnp.bfloat16)

    per_receiver = offsets * cap
    in_row = LANES // per_receiver
    my_row, my_lane = me // in_row, lax.rem(me, in_row) * per_receiver
    block = n_vox * per_dev
    rows = n_vox * cap
    group_rows = 2 * offsets * rows
    span = (2 + offsets) * block
    chunk = 512

    def numbers(part, b, k):
        tiles_in = held[0][part, pl.ds(b * n_vox, n_vox), :, width:].astype(jnp.float32)
        row_id = lax.broadcasted_iota(jnp.int32, tiles_in.shape, 1)
        line = jnp.sum(jnp.where(row_id == my_row, tiles_in, 0.0), axis=1, keepdims=True)
        shape = (n_vox, cap, LANES)
        lane = lax.broadcasted_iota(jnp.int32, shape, 2)
        wanted = lax.broadcasted_iota(jnp.int32, shape, 1) + (my_lane + k * cap)
        picked = jnp.where(lane == wanted, jnp.broadcast_to(line, shape), 0.0)
        return jnp.sum(picked, axis=2, keepdims=True)

    def one_hot(values):
        chosen = lax.broadcasted_iota(jnp.int32, (n_vox, cap, span), 2).astype(jnp.float32)
        hot = jnp.where(chosen == values, 1.0, 0.0)
        return hot.reshape(rows, span).astype(jnp.bfloat16)

    def make_hot(g):
        owner = lax.broadcasted_iota(jnp.int32, (n_vox, cap, 1), 0).astype(jnp.float32) * per_dev
        for u in range(2):
            for k in range(offsets):
                at = pl.multiple_of(g * group_rows + (u * offsets + k) * rows, rows)
                hot_i[pl.ds(at, rows), :] = one_hot(numbers(0, 2 * g + u, k) + owner + u * block)
                hot_j[pl.ds(at, rows), :] = one_hot(numbers(1, 2 * g + u, k) + (u + k + 1) * block)

    def channels(stage, part, g, at):
        found = []
        for u in range(2 + offsets):
            b = lax.rem(2 * g + u, n_chan)
            piece = held[stage][part, pl.ds(b * n_vox, n_vox), :, at : at + chunk]
            found.append(piece.reshape(block, chunk))
        return jnp.concatenate(found, 0)

    def form(stage, passing):
        per_group = width // chunk
        steps = 4 * depth // ((n_chan // 2) * per_group)

        def one_group(g, carry):
            if stage == 0:
                make_hot(g)
            base = pl.multiple_of(g * group_rows, group_rows)
            pick_i, pick_j = hot_i[pl.ds(base, group_rows), :], hot_j[pl.ds(base, group_rows), :]
            total = jnp.zeros((group_rows, table.shape[1]), jnp.float32)
            for c in range(per_group):
                at = c * chunk
                re, im = channels(stage, 0, g, at), channels(stage, 1, g, at)
                re_i = jnp.dot(pick_i, re, preferred_element_type=jnp.float32)
                im_i = jnp.dot(pick_i, im, preferred_element_type=jnp.float32)
                re_j = jnp.dot(pick_j, re, preferred_element_type=jnp.float32)
                im_j = jnp.dot(pick_j, im, preferred_element_type=jnp.float32)
                cross_re = (re_i * re_j + im_i * im_j).astype(jnp.bfloat16)
                cross_im = (im_i * re_j - re_i * im_j).astype(jnp.bfloat16)
                f = stage * width + at
                total += jnp.dot(cross_re, table[f : f + chunk], preferred_element_type=jnp.float32)
                total += jnp.dot(
                    cross_im, table[bins + f : bins + f + chunk], preferred_element_type=jnp.float32
                )
                if passing:
                    step = (g * per_group + c) * steps
                    for phase in range(4):
                        @pl.when(step // depth == phase)
                        def _():
                            for i in range(steps):
                                d = lax.rem(step, depth) + i
                                if phase > 0:
                                    pass_on(stage + 1, phase, d)
                                elif i > 0:
                                    pass_on(stage + 1, 0, d)
                                else:
                                    @pl.when(d > 0)
                                    def _():
                                        pass_on(stage + 1, 0, d)
            if stage > 0:
                total += partial[pl.ds(base, group_rows), :]
            if stage < stages - 1:
                partial[pl.ds(base, group_rows), :] = total
            else:
                for u in range(2):
                    for k in range(offsets):
                        place = pl.multiple_of(k * n_dev * cap + (2 * g + u) * rows, rows)
                        at = (u * offsets + k) * rows
                        lags[pl.ds(place, rows), :] = total[at : at + rows].astype(jnp.bfloat16)
            return carry

        lax.fori_loop(0, n_chan // 2, one_group, 0)

    send_own(0)
    for kind in range(kinds):
        feet_rows[kind * tiles : (kind + 1) * tiles, :] = feet[kind].T
    for phase in range(4):
        def one(d, carry, phase=phase):
            if phase == 0:
                @pl.when(d > 0)
                def _():
                    pass_on(0, 0, d)
            else:
                pass_on(0, phase, d)
            count_piece(phase * depth + d)
            return carry
        lax.fori_loop(0, depth, one, 0)
        if phase == 1:
            for stage in range(1, stages):
                send_own(stage)
    load.wait()
    for stage in range(stages):
        finish_arrivals(stage)
        form(stage, stage + 1 < stages)

    def sent(slot, carry):
        for stage in range(stages):
            for part in range(2):
                copy(stage, part, me, near_core, slot).wait_send()
        return carry

    lax.fori_loop(0, 8 * depth - 1, sent, 0)
    for kind in range(kinds):
        out[kind] = jnp.dot(
            counts[kind * tiles : (kind + 1) * tiles], lags[...], preferred_element_type=jnp.float32
        ).astype(jnp.bfloat16)


def local(spectra, pair_mask, send_rows, footprint, kernels):
    n_chan, n_vox = lax.axis_size("chan"), lax.axis_size("vox")
    n_dev = n_chan * n_vox
    _, per_dev, bins = spectra.shape
    kinds, lag_count, voxels = kernels.shape
    _, offsets, _, cap = send_rows.shape
    tiles, _, slots = footprint.shape
    block = n_vox * per_dev
    table = phase_table(bins, lag_count)
    order = jnp.transpose(send_rows[0], (1, 0, 2))
    own_channel = jnp.where(pair_mask[0][None, :, None] > 0, order // block, -1024)
    numbers = jnp.stack([own_channel, order % block]).reshape(2, per_dev, -1)
    whitened = whiten(spectra)
    stages = 2
    width = bins // stages
    shards = [whitened[:, :, stage * width : (stage + 1) * width] for stage in range(stages)]
    shards[0] = jnp.concatenate([shards[0], numbers.astype(jnp.bfloat16)], -1)
    feet = jnp.transpose(footprint, (1, 2, 0))
    received = offsets * n_dev * cap
    span = (2 + offsets) * block
    vmem = pl.BlockSpec(memory_space=pltpu.VMEM)
    summed = pl.pallas_call(
        functools.partial(kernel, (n_chan, n_vox, per_dev, bins, offsets, cap, stages)),
        out_shape=jax.ShapeDtypeStruct((kinds, tiles, lag_count), jnp.bfloat16),
        in_specs=[vmem] * (stages + 1) + [pl.BlockSpec(memory_space=pl.ANY)],
        out_specs=vmem,
        scratch_shapes=[
            pltpu.VMEM((2, n_dev, per_dev, shard.shape[-1]), jnp.bfloat16) for shard in shards
        ]
        + [
            pltpu.VMEM(table.shape, jnp.bfloat16),
            pltpu.VMEM((kinds * tiles, received), jnp.bfloat16),
            pltpu.VMEM((received, lag_count), jnp.bfloat16),
            pltpu.VMEM((received, lag_count), jnp.float32),
            pltpu.VMEM((kinds * tiles, slots), jnp.int32),
            pltpu.VMEM((received, span), jnp.bfloat16),
            pltpu.VMEM((received, span), jnp.bfloat16),
            pltpu.SemaphoreType.DMA((2 * stages, 8 * n_chan // 2 - 1)),
            pltpu.SemaphoreType.DMA((2 * stages, n_dev)),
            pltpu.SemaphoreType.DMA,
        ],
        compiler_params=pltpu.CompilerParams(
            collective_id=0, has_side_effects=True, vmem_limit_bytes=58 * 1024 * 1024
        ),
    )(*shards, feet, table)
    return lax.dot_general(
        summed, kernels, (((0, 2), (0, 1)), ((), ())), preferred_element_type=jnp.float32
    )


def solution(mesh):
    return jax.shard_map(
        local,
        mesh=mesh,
        in_specs=(
            P(None, ("chan", "vox"), None),
            P("chan", None),
            P(("chan", "vox"), None, None, None),
            P(("chan", "vox"), None, None),
            P(),
        ),
        out_specs=P(("chan", "vox"), None),
        check_vma=False,
    )
```

```python
import functools
import math

import jax
import jax.numpy as jnp
import numpy as np
from jax import lax
from jax.experimental import pallas as pl
from jax.experimental.pallas import tpu as pltpu
from jax.sharding import PartitionSpec as P

MESH = pl.DeviceIdType.MESH
LANES = 128


def whiten(spectra):
    real_part = spectra[0].astype(jnp.float32)
    imag_part = spectra[1].astype(jnp.float32)
    inverse_mag = 1.0 / jnp.sqrt(real_part * real_part + imag_part * imag_part + 0.25)
    return jnp.stack([real_part * inverse_mag, imag_part * inverse_mag]).astype(jnp.bfloat16)


def phase_table(bins, lags):
    bin_index = np.arange(bins, dtype=np.int64)[:, None]
    lag_index = np.arange(lags, dtype=np.int64)[None, :] - lags // 2
    phase_index = bin_index * lag_index % bins
    angles = phase_index.astype(np.float32) * np.float32(2.0 * math.pi / bins)
    norm_factor = np.float32(1.0 / math.sqrt(bins))
    table = np.concatenate([np.cos(angles) * norm_factor, -np.sin(angles) * norm_factor], 0)
    return jnp.asarray(table.astype(jnp.bfloat16))


def kernel(dims, *refs):
    n_chan, n_vox, per_dev, bins, offsets, cap, stages = dims
    own, refs = refs[:stages], refs[stages:]
    feet, table_hbm, out = refs[:3]
    held, refs = refs[3 : 3 + stages], refs[3 + stages :]
    table, counts, lags, partial, feet_rows, hot_i, hot_j, send_sem, recv_sem, load_sem = refs
    n_dev = n_chan * n_vox
    depth = n_chan // 2
    width = bins // stages
    chan, vox = lax.axis_index("chan"), lax.axis_index("vox")
    hi, lo = chan // 2, chan % 2
    far, core = vox // 2, vox % 2
    me = chan * n_vox + vox

    def chan_at(d, flip):
        l = 1 - lo if flip else lo
        return lax.rem(hi + depth - d, depth) * 2 + l

    def vox_at(flip_x, flip_core):
        f = 1 - far if flip_x else far
        c = 1 - core if flip_core else core
        return f * 2 + c

    def source(d, flip_y, flip_x, flip_core):
        return chan_at(d, flip_y) * n_vox + vox_at(flip_x, flip_core)

    barrier = pltpu.get_barrier_semaphore()
    near_y = (chan_at(0, True), vox)
    near_x = (chan, vox_at(True, False))
    near_core = (chan, vox_at(False, True))
    column = [(chan_at(depth - d, False), vox) for d in range(1, depth)]
    partners = column + [near_y, near_x, near_core]
    for device in partners:
        pl.semaphore_signal(barrier, inc=1, device_id=device, device_id_type=MESH)
    for stage in range(stages):
        for part in range(2):
            held[stage][part, me] = own[stage][part]
    load = pltpu.make_async_copy(table_hbm, table, load_sem)
    load.start()
    pl.semaphore_wait(barrier, len(partners))

    first = (near_y, near_x)
    second = (near_x, near_y)

    def copy(stage, part, shard, device, slot):
        return pltpu.make_async_remote_copy(
            src_ref=held[stage].at[part, shard],
            dst_ref=held[stage].at[part, shard],
            send_sem=send_sem.at[stage * 2 + part, slot],
            recv_sem=recv_sem.at[stage * 2 + part, shard],
            device_id=device,
            device_id_type=MESH,
        )

    def spread(stage, part, phase, d, shard):
        if phase == 0:
            copy(stage, part, shard, first[part], d).start()
            copy(stage, part, shard, second[part], depth + d).start()
        if phase == 1:
            copy(stage, part, shard, second[part], 2 * depth + d).start()
        copy(stage, part, shard, near_core, (3 + phase) * depth + d).start()

    def send_own(stage):
        for part in range(2):
            for d, device in enumerate(column):
                copy(stage, part, me, device, 7 * depth + d).start()
        for part in range(2):
            spread(stage, part, 0, 0, me)

    def pass_on(stage, phase, d):
        for part in range(2):
            flip_y = phase == 3 or phase == 1 + part
            flip_x = phase == 3 or phase == 2 - part
            shard = source(d, flip_y, flip_x, False)
            copy(stage, part, shard, near_core, 0).wait_recv()
            spread(stage, part, phase, d, shard)

    def finish_arrivals(stage):
        for flip_y, flip_x in ((False, False), (True, False), (False, True), (True, True)):
            def one(d, carry):
                for part in range(2):
                    shard = source(d, flip_y, flip_x, True)
                    copy(stage, part, shard, near_core, 0).wait_recv()
                return carry
            lax.fori_loop(0, depth, one, 0)

    rows_out, slots = feet_rows.shape
    kinds, tiles = feet.shape[0], feet.shape[2]
    received = counts.shape[1]
    pieces = 4 * depth
    piece_rows = rows_out // pieces

    def count_piece(step):
        start = pl.multiple_of(step * piece_rows, piece_rows)
        slot_id = lax.broadcasted_iota(jnp.int32, (piece_rows, received), 1)
        total = jnp.zeros((piece_rows, received), jnp.float32)
        for slot in range(slots):
            total += jnp.where(slot_id == feet_rows[pl.ds(start, piece_rows), slot : slot + 1], 1.0, 0.0)
        counts[pl.ds(start, piece_rows), :] = total.astype(jnp.bfloat16)

    per_receiver = offsets * cap
    in_row = LANES // per_receiver
    my_row, my_lane = me // in_row, lax.rem(me, in_row) * per_receiver
    block = n_vox * per_dev
    rows = n_vox * cap
    group_rows = 2 * offsets * rows
    span = (2 + offsets) * block
    chunk = 512

    def numbers(part, b, k):
        tiles_in = held[0][part, pl.ds(b * n_vox, n_vox), :, width:].astype(jnp.float32)
        row_id = lax.broadcasted_iota(jnp.int32, tiles_in.shape, 1)
        line = jnp.sum(jnp.where(row_id == my_row, tiles_in, 0.0), axis=1, keepdims=True)
        shape = (n_vox, cap, LANES)
        lane = lax.broadcasted_iota(jnp.int32, shape, 2)
        wanted = lax.broadcasted_iota(jnp.int32, shape, 1) + (my_lane + k * cap)
        picked = jnp.where(lane == wanted, jnp.broadcast_to(line, shape), 0.0)
        return jnp.sum(picked, axis=2, keepdims=True)

    def one_hot(values):
        chosen = lax.broadcasted_iota(jnp.int32, (n_vox, cap, span), 2).astype(jnp.float32)
        hot = jnp.where(chosen == values, 1.0, 0.0)
        return hot.reshape(rows, span).astype(jnp.bfloat16)

    def make_hot(g):
        owner = lax.broadcasted_iota(jnp.int32, (n_vox, cap, 1), 0).astype(jnp.float32) * per_dev
        for u in range(2):
            for k in range(offsets):
                at = pl.multiple_of(g * group_rows + (u * offsets + k) * rows, rows)
                hot_i[pl.ds(at, rows), :] = one_hot(numbers(0, 2 * g + u, k) + owner + u * block)
                hot_j[pl.ds(at, rows), :] = one_hot(numbers(1, 2 * g + u, k) + (u + k + 1) * block)

    def channels(stage, part, g, at):
        found = []
        for u in range(2 + offsets):
            b = lax.rem(2 * g + u, n_chan)
            piece = held[stage][part, pl.ds(b * n_vox, n_vox), :, at : at + chunk]
            found.append(piece.reshape(block, chunk))
        return jnp.concatenate(found, 0)

    def form(stage, passing):
        per_group = width // chunk
        steps = 2 * depth // ((n_chan // 2) * per_group)

        def one_group(g, carry):
            if stage == 0:
                make_hot(g)
            base = pl.multiple_of(g * group_rows, group_rows)
            pick_i, pick_j = hot_i[pl.ds(base, group_rows), :], hot_j[pl.ds(base, group_rows), :]
            total = jnp.zeros((group_rows, table.shape[1]), jnp.float32)
            for c in range(per_group):
                at = c * chunk
                re, im = channels(stage, 0, g, at), channels(stage, 1, g, at)
                re_i = jnp.dot(pick_i, re, preferred_element_type=jnp.float32).astype(jnp.bfloat16)
                im_i = jnp.dot(pick_i, im, preferred_element_type=jnp.float32).astype(jnp.bfloat16)
                re_j = jnp.dot(pick_j, re, preferred_element_type=jnp.float32).astype(jnp.bfloat16)
                im_j = jnp.dot(pick_j, im, preferred_element_type=jnp.float32).astype(jnp.bfloat16)
                cross_re = (re_i * re_j + im_i * im_j).astype(jnp.bfloat16)
                cross_im = (im_i * re_j - re_i * im_j).astype(jnp.bfloat16)
                f = stage * width + at
                total += jnp.dot(cross_re, table[f : f + chunk], preferred_element_type=jnp.float32)
                total += jnp.dot(
                    cross_im, table[bins + f : bins + f + chunk], preferred_element_type=jnp.float32
                )
                if passing:
                    step = (g * per_group + c) * steps
                    for phase in (2, 3):
                        @pl.when(step // depth == phase - 2)
                        def _():
                            for i in range(steps):
                                pass_on(stage + 1, phase, lax.rem(step, depth) + i)
            if stage > 0:
                total += partial[pl.ds(base, group_rows), :]
            if stage < stages - 1:
                partial[pl.ds(base, group_rows), :] = total
            else:
                for u in range(2):
                    for k in range(offsets):
                        place = pl.multiple_of(k * n_dev * cap + (2 * g + u) * rows, rows)
                        at = (u * offsets + k) * rows
                        lags[pl.ds(place, rows), :] = total[at : at + rows].astype(jnp.bfloat16)
            return carry

        lax.fori_loop(0, n_chan // 2, one_group, 0)

    send_own(0)
    for kind in range(kinds):
        feet_rows[kind * tiles : (kind + 1) * tiles, :] = feet[kind].T
    for phase in range(4):
        def one(d, carry, phase=phase):
            if phase == 0:
                @pl.when(d > 0)
                def _():
                    pass_on(0, 0, d)
            else:
                pass_on(0, phase, d)
            if phase == 2:
                @pl.when(d > 0)
                def _():
                    pass_on(1, 0, d)
            if phase == 3:
                pass_on(1, 1, d)
            count_piece(phase * depth + d)
            return carry
        lax.fori_loop(0, depth, one, 0)
        if phase == 1:
            for stage in range(1, stages):
                send_own(stage)
    load.wait()
    for stage in range(stages):
        finish_arrivals(stage)
        form(stage, stage + 1 < stages)

    def sent(slot, carry):
        for stage in range(stages):
            for part in range(2):
                copy(stage, part, me, near_core, slot).wait_send()
        return carry

    lax.fori_loop(0, 8 * depth - 1, sent, 0)
    for kind in range(kinds):
        out[kind] = jnp.dot(
            counts[kind * tiles : (kind + 1) * tiles], lags[...], preferred_element_type=jnp.float32
        ).astype(jnp.bfloat16)


def local(spectra, pair_mask, send_rows, footprint, kernels):
    n_chan, n_vox = lax.axis_size("chan"), lax.axis_size("vox")
    n_dev = n_chan * n_vox
    _, per_dev, bins = spectra.shape
    kinds, lag_count, voxels = kernels.shape
    _, offsets, _, cap = send_rows.shape
    tiles, _, slots = footprint.shape
    block = n_vox * per_dev
    table = phase_table(bins, lag_count)
    order = jnp.transpose(send_rows[0], (1, 0, 2))
    own_channel = jnp.where(pair_mask[0][None, :, None] > 0, order // block, -1024)
    numbers = jnp.stack([own_channel, order % block]).reshape(2, per_dev, -1)
    whitened = whiten(spectra)
    stages = 2
    width = bins // stages
    shards = [whitened[:, :, stage * width : (stage + 1) * width] for stage in range(stages)]
    shards[0] = jnp.concatenate([shards[0], numbers.astype(jnp.bfloat16)], -1)
    feet = jnp.transpose(footprint, (1, 2, 0))
    received = offsets * n_dev * cap
    span = (2 + offsets) * block
    vmem = pl.BlockSpec(memory_space=pltpu.VMEM)
    summed = pl.pallas_call(
        functools.partial(kernel, (n_chan, n_vox, per_dev, bins, offsets, cap, stages)),
        out_shape=jax.ShapeDtypeStruct((kinds, tiles, lag_count), jnp.bfloat16),
        in_specs=[vmem] * (stages + 1) + [pl.BlockSpec(memory_space=pl.ANY)],
        out_specs=vmem,
        scratch_shapes=[
            pltpu.VMEM((2, n_dev, per_dev, shard.shape[-1]), jnp.bfloat16) for shard in shards
        ]
        + [
            pltpu.VMEM(table.shape, jnp.bfloat16),
            pltpu.VMEM((kinds * tiles, received), jnp.bfloat16),
            pltpu.VMEM((received, lag_count), jnp.bfloat16),
            pltpu.VMEM((received, lag_count), jnp.float32),
            pltpu.VMEM((kinds * tiles, slots), jnp.int32),
            pltpu.VMEM((received, span), jnp.bfloat16),
            pltpu.VMEM((received, span), jnp.bfloat16),
            pltpu.SemaphoreType.DMA((2 * stages, 8 * n_chan // 2 - 1)),
            pltpu.SemaphoreType.DMA((2 * stages, n_dev)),
            pltpu.SemaphoreType.DMA,
        ],
        compiler_params=pltpu.CompilerParams(
            collective_id=0, has_side_effects=True, vmem_limit_bytes=58 * 1024 * 1024
        ),
    )(*shards, feet, table)
    return lax.dot_general(
        summed, kernels, (((0, 2), (0, 1)), ((), ())), preferred_element_type=jnp.float32
    )


def solution(mesh):
    return jax.shard_map(
        local,
        mesh=mesh,
        in_specs=(
            P(None, ("chan", "vox"), None),
            P("chan", None),
            P(("chan", "vox"), None, None, None),
            P(("chan", "vox"), None, None),
            P(),
        ),
        out_specs=P(("chan", "vox"), None),
        check_vma=False,
    )
```
